32 devices in a mesh: grp: 2 (over x), yz: 8 (over z, y), gx: 2 (over core).
Axes of the slice: x: 2, y: 2, z: 4, core: 2. Of those that a mesh axis runs over, the one named last changes fastest.
Arguments:
- hidden: bfloat16 [2, 192, 16384], P(None, ('grp', 'yz'), 'gx'), parts along dimension 1, may hold values from -6 to 6
- w_query: bfloat16 [16384, 8192], P('gx', 'yz'), may hold values from -0.046875 to 0.046875
- key_value_weight: bfloat16 [16384, 1024], P('gx', 'yz'), may hold values from -0.046875 to 0.046875
- w_out: bfloat16 [8192, 16384], P('gx', 'yz'), may hold values from -0.125 to 0.125
- cache_keys: bfloat16 [192, 4, 512, 128], P(('grp', 'yz'), 'gx'), parts along dimension 0, may hold values from -64 to 64
- stored_values: bfloat16 [192, 4, 512, 128], P(('grp', 'yz'), 'gx'), parts along dimension 0, may hold values from -6 to 6
- lengths: int32 [192], P(('grp', 'yz')), parts along dimension 0, may hold values from 1 to 512, 19660 in all
- positions: int32 [192], P(('grp', 'yz')), parts along dimension 0, may hold values from 0 to 8191
Outputs:
- attention_out: bfloat16 [2, 192, 16384], P(None, 'grp', ('yz', 'gx')), parts along dimension 1
- new_entries: bfloat16 [2, 192, 4, 2, 128], P(None, ('grp', 'yz'), 'gx'), parts along dimension 1
The draws below stay inside these ranges and needn't reach their ends.
There are 2 independent parts, one for each index of `grp`. The reference program is written for one: setup_inputs(seed, part) draws one part's arguments, and reference() takes and returns one part's arrays. A program takes and returns all parts, laid end to end along the dimension named above; an argument that names none is the same for every part. Nothing has to cross between parts.
Inputs may be any that keep to these rules, and one draw needn't show every extreme that they name: Row b's caches hold lengths[b] filled slots at the front; in every draw some row fills all 512.
All inputs are finite; a program needn't handle non-finite values. No bound on the sum of `lengths` on one device may be relied on, other than what follows from the above.
Results may differ from the reference program's by a relative error of at most 0.009.
Values may be sent and summed in bfloat16 or wider, within the bound.
A program may use at most 256 MiB of HBM per device.

```python
import math
import jax
import jax.numpy as jnp
import numpy as np

MODEL_DIM = 16384
HEAD_SIZE = 128
HQ = 64
KEY_VALUE_HEADS = 4
STEPS = 2
CACHE_SLOTS = 512
BATCH_ROWS = 96


def draw_cache_keys(key, part):
    key = jax.random.fold_in(key, 7)
    key_base = jax.random.fold_in(key, 0)
    complete_shape = (BATCH_ROWS, KEY_VALUE_HEADS, CACHE_SLOTS, HEAD_SIZE)
    values = jax.random.truncated_normal(key_base, -6.0, 6.0, complete_shape, jnp.float32)
    return values.astype(jnp.bfloat16)


def touch_ends(drawn, own_key, least, high):
    shape = drawn.shape
    index_at = [jax.random.randint(jax.random.fold_in(own_key, axis), (), 0, shape[axis]) for axis in range(len(shape))]
    drawn = drawn.at[tuple(index_at)].set(least)
    longest = shape.index(max(shape))
    index_at[longest] = (index_at[longest] + 1) % shape[longest]
    return drawn.at[tuple(index_at)].set(high)


def block_levels(key, dims, pieces, least, top_value):
    factor_of = 1.0
    for dim, parts in pieces:
        heights = jax.random.uniform(jax.random.fold_in(jax.random.fold_in(key, 6), dim), (parts,), jnp.float32, least / len(pieces), top_value / len(pieces))
        factor_of = factor_of * jnp.repeat(jnp.exp(heights), dims[dim] // parts).reshape((-1,) + (1,) * (len(dims) - 1 - dim))
    return factor_of


def profile(number_of, total, bound, lean):
    loads = [(1 << 20) // math.isqrt(rank ** lean) + 1 for rank in range(2, number_of + 1)]
    surplus, counts = total - bound - (number_of - 1), [1] * (number_of - 1)
    while surplus > 0:
        movable = [i for i in range(number_of - 1) if counts[i] < bound]
        pool, remaining = sum([loads[i] for i in movable]), surplus
        for i in movable:
            extra = min(bound - counts[i], max(1, remaining * loads[i] // pool), surplus)
            counts[i] = counts[i] + extra
            surplus = surplus - extra
    return np.array([bound] + counts)


def ragged_sizes(own_key, count, total, limit, lean):
    if count == 2:
        one = jax.random.randint(own_key, (), max(1, total - limit), min(limit, total - 1) + 1)
        return jnp.stack([one, total - one])
    tallies = jnp.asarray(profile(count, total, limit, lean), jnp.int32)
    pairs = (count - 1) // 2
    source_of, taker = tallies[1:1 + 2 * pairs:2], tallies[2:2 + 2 * pairs:2]
    slack = jnp.minimum(source_of - 1, limit - taker)
    shifted = jax.random.randint(jax.random.fold_in(own_key, 1), (pairs,), 0, 1 << 20) % (slack + 1)
    tallies = tallies.at[1:1 + 2 * pairs:2].set(source_of - shifted).at[2:2 + 2 * pairs:2].set(taker + shifted)
    return tallies[jax.random.permutation(jax.random.fold_in(own_key, 2), count)]


def scatter_about(stream_key, dims, deviation, reach, cuts=(), held_as=jnp.bfloat16):
    drawn = deviation * jax.random.normal(stream_key, dims, jnp.float32)
    if cuts:
        drawn = drawn * block_levels(stream_key, dims, cuts, -0.22, 0.18)
    return jnp.clip(drawn, -reach, reach).astype(held_as)


def setup_inputs(seed: int = 0, part: int = 0) -> dict:
    streams_of = jax.random.split(jax.random.key(seed), 9)
    own_keys = jax.random.split(jax.random.fold_in(streams_of[8], part), 9)
    return {
        "hidden": scatter_about(own_keys[0], (STEPS, BATCH_ROWS, MODEL_DIM), 1.0, 6.0, ((1, 8), (2, 2))),
        "w_query": scatter_about(streams_of[1], (MODEL_DIM, HQ * HEAD_SIZE), MODEL_DIM ** -0.5, 0.046875, ((0, 2), (1, 8))),
        "key_value_weight": scatter_about(streams_of[2], (MODEL_DIM, 2 * KEY_VALUE_HEADS * HEAD_SIZE), MODEL_DIM ** -0.5, 0.046875, ((0, 2), (1, 8))),
        "w_out": scatter_about(streams_of[3], (HQ * HEAD_SIZE, MODEL_DIM), (HQ * HEAD_SIZE // 4) ** -0.5, 0.125, ((0, 2), (1, 8))),
        "cache_keys": draw_cache_keys(jax.random.fold_in(jax.random.fold_in(streams_of[8], part), 71), part),
        "stored_values": scatter_about(own_keys[5], (BATCH_ROWS, KEY_VALUE_HEADS, CACHE_SLOTS, HEAD_SIZE), 1.0, 6.0, ((0, 8), (1, 2))),
        "lengths": ragged_sizes(own_keys[6], BATCH_ROWS, BATCH_ROWS * CACHE_SLOTS * 2 // 5, CACHE_SLOTS, 2).astype(jnp.int32),
        "positions": touch_ends(jax.random.randint(own_keys[7], (BATCH_ROWS,), 0, 8192), jax.random.fold_in(own_keys[7], 1), 0, 8191).astype(jnp.int32),
    }


def rotary(vector, position):
    half_dim = vector.shape[-1] // 2
    freq_index = jnp.arange(half_dim, dtype=jnp.float32)
    inverse_freq = jnp.exp(freq_index * (-2.0 * math.log(500000.0) / vector.shape[-1]))
    phase_angle = position.astype(jnp.float32)[..., None] * inverse_freq
    cosine = jnp.cos(phase_angle)
    sine_part = jnp.sin(phase_angle)
    lower_half = vector[..., :half_dim]
    upper_half = vector[..., half_dim:]
    return jnp.concatenate([lower_half * cosine - upper_half * sine_part, upper_half * cosine + lower_half * sine_part], axis=-1)


def reference(hidden, w_query, key_value_weight, w_out, cache_keys, stored_values, lengths, positions):
    step_count, row_count, model_width = hidden.shape
    head_count = w_query.shape[1] // HEAD_SIZE
    kv_count = key_value_weight.shape[1] // (2 * HEAD_SIZE)
    group_size = head_count // kv_count
    flat_rows = hidden.reshape(step_count * row_count, model_width)
    query_proj = jnp.dot(flat_rows, w_query, preferred_element_type=jnp.float32).reshape(step_count, row_count, head_count, HEAD_SIZE)
    fresh_proj = jnp.dot(flat_rows, key_value_weight, preferred_element_type=jnp.float32).reshape(step_count, row_count, kv_count, 2, HEAD_SIZE)
    step_pos = positions[None, :] + jnp.arange(step_count, dtype=jnp.int32)[:, None]
    rotated_query = rotary(query_proj, step_pos[:, :, None]).astype(jnp.bfloat16)
    new_key = rotary(fresh_proj[:, :, :, 0], step_pos[:, :, None])
    new_entries = jnp.stack([new_key, fresh_proj[:, :, :, 1]], axis=3).astype(jnp.bfloat16)
    grouped = rotated_query.reshape(step_count, row_count, kv_count, group_size, HEAD_SIZE).astype(jnp.float32)
    score_scale = HEAD_SIZE ** -0.5
    cache_scores = jnp.einsum('sbhgd,bhld->sbhgl', grouped, cache_keys.astype(jnp.float32)) * score_scale
    slot_valid = jnp.arange(CACHE_SLOTS)[None, :] < lengths[:, None]
    cache_scores = jnp.where(slot_valid[None, :, None, None, :], cache_scores, -jnp.inf)
    entries_wide = new_entries.astype(jnp.float32)
    new_scores = jnp.einsum('sbhgd,tbhd->sbhgt', grouped, entries_wide[:, :, :, 0]) * score_scale
    step_valid = jnp.arange(step_count)[None, :] <= jnp.arange(step_count)[:, None]
    new_scores = jnp.where(step_valid[:, None, None, None, :], new_scores, -jnp.inf)
    row_top = jnp.maximum(jnp.max(cache_scores, axis=4), jnp.max(new_scores, axis=4))[..., None]
    cache_exp = jnp.exp(cache_scores - row_top)
    new_exp = jnp.exp(new_scores - row_top)
    denominator = jnp.sum(cache_exp, axis=4, keepdims=True) + jnp.sum(new_exp, axis=4, keepdims=True)
    cache_weights = (cache_exp / denominator).astype(jnp.bfloat16)
    new_weights = (new_exp / denominator).astype(jnp.bfloat16)
    attended = jnp.einsum('sbhgl,bhld->sbhgd', cache_weights.astype(jnp.float32), stored_values.astype(jnp.float32))
    attended = attended + jnp.einsum('sbhgt,tbhd->sbhgd', new_weights.astype(jnp.float32), entries_wide[:, :, :, 1])
    attended = attended.astype(jnp.bfloat16).reshape(step_count * row_count, head_count * HEAD_SIZE)
    attention_out = jnp.dot(attended, w_out, preferred_element_type=jnp.float32).astype(jnp.bfloat16)
    return attention_out.reshape(step_count, row_count, model_width), new_entries
```

```python
import functools
import math

import jax
import jax.numpy as jnp
from jax import lax
from jax.experimental import pallas as pl
from jax.experimental.pallas import tpu as pltpu
from jax.sharding import PartitionSpec as P

MESH = pl.DeviceIdType.MESH
VMEM_BYTES = 56 * 1024 * 1024


def remote(src, dst, send, recv, **where):
    return pltpu.make_async_remote_copy(
        src_ref=src, dst_ref=dst, send_sem=send, recv_sem=recv, device_id=where, device_id_type=MESH
    )


def enter(n):
    me, core = lax.axis_index("yz"), lax.axis_index("gx")
    barrier = pltpu.get_barrier_semaphore()
    for k in range(1, 2 * n):
        there = lax.rem(me * 2 + core + k, 2 * n)
        pl.semaphore_signal(
            barrier,
            inc=1,
            device_id={"yz": lax.div(there, 2), "gx": lax.rem(there, 2)},
            device_id_type=MESH,
        )
    pl.semaphore_wait(barrier, 2 * n - 1)


class Gather:
    def __init__(self, ny, n, x, xg, own, send, recv):
        self.ny, self.nz, self.n = ny, n // ny, n
        self.x, self.xg, self.own, self.send, self.recv = x, xg, own, send, recv
        self.me = lax.axis_index("yz")
        self.z, self.y = lax.div(self.me, ny), lax.rem(self.me, ny)
        self.chunks = x.shape[0]

    def load(self, c):
        return pltpu.make_async_copy(self.x.at[c], self.xg.at[c, self.me], self.own.at[c])

    def copy(self, c, d, way):
        to = {0: self.me + 1 - 2 * self.y, 1: self.me + self.ny, 2: self.me - self.ny}[way]
        block = self.xg.at[c, d]
        return remote(block, block, self.send.at[c, d, way], self.recv.at[c, d], yz=to)

    def await_block(self, c, d):
        block = self.xg.at[c, d]
        remote(block, block, self.send.at[c, d, 0], self.recv.at[c, d], yz=self.me).wait_recv()

    def ways(self, c, act):
        self.own_sends(c, act)
        for s in range(1, self.nz):
            self.hop_sends(c, s, 1, act)
            self.hop_sends(c, s, -1, act)

    def own_sends(self, c, act):
        @pl.when(self.z + 1 < self.nz)
        def _():
            act(self.copy(c, self.me, 1))

        @pl.when(self.z > 0)
        def _():
            act(self.copy(c, self.me, 2))

        if self.ny == 2:
            act(self.copy(c, self.me, 0))

    def hop_sends(self, c, s, sign, act, first=None):
        origin = self.z - sign * s
        d = origin * self.ny + self.y

        @pl.when((origin >= 0) & (origin < self.nz))
        def _():
            if first is not None:
                first(d)
            onward = self.z + sign

            @pl.when((onward >= 0) & (onward < self.nz))
            def _():
                act(self.copy(c, d, 1 if sign > 0 else 2))

            if self.ny == 2:
                act(self.copy(c, d, 0))

    def begin(self, c):
        self.load(c).wait()
        self.own_sends(c, lambda copy: copy.start())

    def pass_on(self, c):
        for s in range(1, self.nz):
            for sign in (1, -1):
                self.hop_sends(
                    c, s, sign, lambda copy: copy.start(), lambda d: self.await_block(c, d)
                )

    def across(self, c):
        if self.ny == 2:
            for z in range(self.nz):
                self.await_block(c, z * 2 + 1 - self.y)

    def finish(self):
        for c in range(self.chunks):
            self.ways(c, lambda copy: copy.wait_send())

    def run(self, compute):
        for c in range(self.chunks):
            self.load(c).start()
        enter(self.n)
        self.begin(0)
        for c in range(self.chunks):
            if c + 1 < self.chunks:
                self.begin(c + 1)
            self.pass_on(c)
            if c > 0:
                self.across(c - 1)
                compute(c - 1)
        self.across(self.chunks - 1)
        compute(self.chunks - 1)


def rows_of(xg, c, first, count, half):
    rows = xg.shape[2] // 2
    block = xg[c, pl.ds(first, count)]
    block = block.astype(jnp.float32)[:, half * rows : (half + 1) * rows, :]
    return block.reshape(count * rows, xg.shape[3]).astype(jnp.bfloat16)


def project_kernel(
    ny, n, x, tab, w_q, w_kv, q_out, kv_out,
    xg, tabs, wq, wkv, acc_q, acc_kv, got_q, got_kv, q_send, kv_send, q_recv, kv_recv,
    own, send, recv, w_sem, t_send, t_recv, p_send, p_recv, a_send, a_recv,
):
    me, core = lax.axis_index("yz"), lax.axis_index("gx")
    half = n // 2
    chunks, kc = x.shape[0], x.shape[2]
    rows = x.shape[1] // 2
    depth = w_q.shape[0]
    mine, other = core * half, (1 - core) * half
    side = lax.div(me, half)

    def weight(c, h, which):
        part = pl.ds(h * (depth // 2) + c * kc, kc)
        src, dst = ((w_q, wq), (w_kv, wkv))[which]
        return pltpu.make_async_copy(src.at[part], dst.at[part], w_sem.at[c, h, which])

    for c in range(chunks):
        for h in range(2):
            for which in range(2):
                weight(c, h, which).start()

    gather = Gather(ny, n, x, xg, own, send, recv)

    def tab_copy(k):
        to = lax.rem(me + k, n)
        return remote(tab, tabs.at[lax.rem(me, half)], t_send.at[k - 1], t_recv.at[lax.rem(me, half)], yz=to)

    def product(c, first, at):
        total_q = total_kv = None
        for h in range(2):
            part = pl.ds(h * (depth // 2) + c * kc, kc)
            lhs = rows_of(xg, c, first, half, h)
            term_q = jnp.dot(lhs, wq[part, :], preferred_element_type=jnp.float32)
            term_kv = jnp.dot(lhs, wkv[part, :], preferred_element_type=jnp.float32)
            total_q = term_q if h == 0 else total_q + term_q
            total_kv = term_kv if h == 0 else total_kv + term_kv
        if c == 0:
            acc_q[at] = total_q
            acc_kv[at] = total_kv
        else:
            acc_q[at] += total_q
            acc_kv[at] += total_kv

    swap_q = remote(acc_q.at[1], got_q, p_send.at[0], p_recv.at[0], gx=1 - core)
    swap_kv = remote(acc_kv.at[1], got_kv, p_send.at[1], p_recv.at[1], gx=1 - core)

    def compute(c):
        for h in range(2):
            for which in range(2):
                weight(c, h, which).wait()
        if c == 0:
            @pl.when(side == core)
            def _():
                tabs[lax.rem(me, half)] = tab[...]
                for k in range(1, n):
                    tab_copy(k).start()
        product(c, other, 1)
        if c == chunks - 1:
            swap_q.start()
            swap_kv.start()
        product(c, mine, 0)

    gather.run(compute)

    for i in range(half):
        @pl.when(mine + i != me)
        def _():
            remote(tab, tabs.at[i], t_send.at[0], t_recv.at[i], yz=me).wait_recv()

    swap_q.wait_recv()
    swap_kv.wait_recv()
    heads = wq.shape[1] // 128

    def q_copy(i):
        return remote(
            q_send.at[i], q_recv.at[lax.rem(me, half)], a_send.at[0, i], a_recv.at[0, lax.rem(me, half)],
            yz=mine + i, gx=side,
        )

    def kv_copy(i):
        return remote(
            kv_send.at[i], kv_recv.at[lax.rem(me, half)], a_send.at[1, i], a_recv.at[1, lax.rem(me, half)],
            yz=mine + i, gx=side,
        )

    for i in range(half):
        part = slice(i * rows, (i + 1) * rows)
        cosine = tabs[i, :, :128]
        sine = tabs[i, :, 128:]
        turned = []
        for head in range(heads):
            cols = slice(head * 128, (head + 1) * 128)
            u = acc_q[0, part, cols] + got_q[part, cols]
            turned.append(u * cosine + pltpu.roll(u, 64, 1) * sine)
            if head % 2 == 1:
                pair = jnp.concatenate(turned[-2:], axis=0).astype(jnp.bfloat16)
                q_send[i, pl.ds((head - 1) * rows, 2 * rows), :] = pair
        kv_send[i] = acc_kv[0, part, :] + got_kv[part, :]
        here = (mine + i == me) & (side == core)

        @pl.when(jnp.logical_not(here))
        def _():
            q_copy(i).start()
            kv_copy(i).start()

        @pl.when(here)
        def _():
            q_recv[lax.rem(me, half)] = q_send[i]
            kv_recv[lax.rem(me, half)] = kv_send[i]

    for j in range(half):
        @pl.when(jnp.logical_not((mine + j == me) & (side == core)))
        def _():
            remote(q_send.at[0], q_recv.at[j], a_send.at[0, 0], a_recv.at[0, j], yz=me).wait_recv()
            remote(kv_send.at[0], kv_recv.at[j], a_send.at[1, 0], a_recv.at[1, j], yz=me).wait_recv()

    q_out[...] = q_recv[...]
    kv_out[...] = kv_recv[...]

    gather.finish()
    swap_q.wait_send()
    swap_kv.wait_send()

    @pl.when(side == core)
    def _():
        for k in range(1, n):
            tab_copy(k).wait_send()

    for i in range(half):
        @pl.when(jnp.logical_not((mine + i == me) & (side == core)))
        def _():
            q_copy(i).wait_send()
            kv_copy(i).wait_send()


def project(ny, n, x, tab, w_q, w_kv):
    chunks, rows2, kc = x.shape
    rows, half = rows2 // 2, n // 2
    depth, qcols = w_q.shape
    kvcols = w_kv.shape[1]
    heads = qcols // 128
    f32, bf16 = jnp.float32, jnp.bfloat16
    dma = pltpu.SemaphoreType.DMA
    vmem = pl.BlockSpec(memory_space=pltpu.VMEM)
    hbm = pl.BlockSpec(memory_space=pl.ANY)
    return pl.pallas_call(
        functools.partial(project_kernel, ny, n),
        out_shape=(
            jax.ShapeDtypeStruct((half, heads * rows, 128), bf16),
            jax.ShapeDtypeStruct((half, rows, kvcols), f32),
        ),
        in_specs=[hbm, vmem, hbm, hbm],
        out_specs=(vmem, vmem),
        scratch_shapes=[
            pltpu.VMEM((chunks, n, rows2, kc), bf16),
            pltpu.VMEM((half, rows, 256), f32),
            pltpu.VMEM((depth, qcols), bf16),
            pltpu.VMEM((depth, kvcols), bf16),
            pltpu.VMEM((2, half * rows, qcols), f32),
            pltpu.VMEM((2, half * rows, kvcols), f32),
            pltpu.VMEM((half * rows, qcols), f32),
            pltpu.VMEM((half * rows, kvcols), f32),
            pltpu.VMEM((half, heads * rows, 128), bf16),
            pltpu.VMEM((half, rows, kvcols), f32),
            pltpu.VMEM((half, heads * rows, 128), bf16),
            pltpu.VMEM((half, rows, kvcols), f32),
            dma((chunks,)),
            dma((chunks, n, 3)),
            dma((chunks, n)),
            dma((chunks, 2, 2)),
            dma((n - 1,)),
            dma((half,)),
            dma((2,)),
            dma((2,)),
            dma((2, half)),
            dma((2, half)),
        ],
        compiler_params=pltpu.CompilerParams(
            collective_id=0, has_side_effects=True, vmem_limit_bytes=VMEM_BYTES
        ),
        cost_estimate=pl.CostEstimate(
            flops=2 * n * rows * depth * (qcols + kvcols),
            bytes_accessed=2 * depth * (qcols + kvcols),
            transcendentals=0,
        ),
    )(x, tab, w_q, w_kv)


def mix_kernel(ny, n, x, w, out, xg, wv, acc, got, own, send, recv, w_sem, p_send, p_recv):
    core = lax.axis_index("gx")
    chunks, kc = x.shape[0], x.shape[2]
    depth, cols = w.shape[0], w.shape[1] // 2

    def weight(c, h):
        part = pl.ds(h * (depth // 2) + c * kc, kc)
        return pltpu.make_async_copy(w.at[part], wv.at[part], w_sem.at[c, h])

    for c in range(chunks):
        for h in range(2):
            weight(c, h).start()

    gather = Gather(ny, n, x, xg, own, send, recv)
    swap = remote(acc.at[1], got, p_send.at[0], p_recv.at[0], gx=1 - core)

    def product(c, lhs, first, at):
        columns = pl.ds(pl.multiple_of(first, 128), cols)
        total = None
        for h in range(2):
            part = pl.ds(h * (depth // 2) + c * kc, kc)
            term = jnp.dot(lhs[h], wv[part, columns], preferred_element_type=jnp.float32)
            total = term if h == 0 else total + term
        if c == 0:
            acc[at] = total
        else:
            acc[at] += total

    def compute(c):
        for h in range(2):
            weight(c, h).wait()
        lhs = [rows_of(xg, c, 0, n, h) for h in range(2)]
        product(c, lhs, (1 - core) * cols, 1)
        if c == chunks - 1:
            swap.start()
        product(c, lhs, core * cols, 0)

    gather.run(compute)
    swap.wait_recv()
    out[...] = (acc[0] + got[...]).astype(out.dtype)
    gather.finish()
    swap.wait_send()


def mix(ny, n, x, w):
    chunks, rows2, kc = x.shape
    total = n * rows2 // 2
    depth, width = w.shape
    f32, bf16 = jnp.float32, jnp.bfloat16
    dma = pltpu.SemaphoreType.DMA
    vmem = pl.BlockSpec(memory_space=pltpu.VMEM)
    hbm = pl.BlockSpec(memory_space=pl.ANY)
    return pl.pallas_call(
        functools.partial(mix_kernel, ny, n),
        out_shape=jax.ShapeDtypeStruct((total, width // 2), bf16),
        in_specs=[hbm, hbm],
        out_specs=vmem,
        scratch_shapes=[
            pltpu.VMEM((chunks, n, rows2, kc), bf16),
            pltpu.VMEM((depth, width), bf16),
            pltpu.VMEM((2, total, width // 2), f32),
            pltpu.VMEM((total, width // 2), f32),
            dma((chunks,)),
            dma((chunks, n, 3)),
            dma((chunks, n)),
            dma((chunks, 2)),
            dma((1,)),
            dma((1,)),
        ],
        compiler_params=pltpu.CompilerParams(
            collective_id=1, has_side_effects=True, vmem_limit_bytes=VMEM_BYTES
        ),
        cost_estimate=pl.CostEstimate(
            flops=2 * total * depth * width, bytes_accessed=2 * depth * width, transcendentals=0
        ),
    )(x, w)


def attend_kernel(lengths, q, entries, keys, values, out):
    per_step, kv_local, query_rows, head_dim = q.shape
    slots = keys.shape[2]
    scale = head_dim ** (-0.5)
    f32 = jnp.float32
    base = pl.program_id(0) * per_step
    slot = lax.broadcasted_iota(jnp.int32, (query_rows, slots), 1)
    first = lax.broadcasted_iota(jnp.int32, (query_rows, 1), 0) < query_rows // 2
    for b in range(per_step):
        valid = slot < lengths[base + b]
        for h in range(kv_local):
            query = q[b, h]
            scores = lax.dot_general(
                query, keys[b, h], (((1,), (1,)), ((), ())), preferred_element_type=f32
            ) * scale
            scores = jnp.where(valid, scores, -jnp.inf)
            wide = query.astype(f32)
            fresh = entries[b, h]
            new0 = jnp.sum(wide * fresh[0:1], axis=1, keepdims=True) * scale
            new1 = jnp.sum(wide * fresh[1:2], axis=1, keepdims=True) * scale
            new1 = jnp.where(first, -jnp.inf, new1)
            top = jnp.maximum(jnp.max(scores, axis=1, keepdims=True), jnp.maximum(new0, new1))
            grown = jnp.exp(scores - top)
            grown0, grown1 = jnp.exp(new0 - top), jnp.exp(new1 - top)
            total = jnp.sum(grown, axis=1, keepdims=True) + (grown0 + grown1)
            weights = (grown / total).astype(jnp.bfloat16)
            weight0 = (grown0 / total).astype(jnp.bfloat16).astype(f32)
            weight1 = (grown1 / total).astype(jnp.bfloat16).astype(f32)
            result = jnp.dot(weights, values[b, h], preferred_element_type=f32)
            result = result + (weight0 * fresh[2:3] + weight1 * fresh[3:4])
            out[b, h] = result.astype(out.dtype)


def attend(lengths, q, entries, keys, values):
    rows, kv_local, query_rows, head_dim = q.shape
    slots = keys.shape[2]
    per_step = next(k for k in (3, 4, 2, 1) if rows % k == 0)

    def block(*shape):
        return pl.BlockSpec((per_step, *shape), lambda i: (i,) + (0,) * len(shape))

    return pl.pallas_call(
        attend_kernel,
        grid=(rows // per_step,),
        out_shape=jax.ShapeDtypeStruct(q.shape, jnp.bfloat16),
        in_specs=[
            pl.BlockSpec(memory_space=pltpu.SMEM),
            block(kv_local, query_rows, head_dim),
            block(kv_local, entries.shape[2], head_dim),
            block(kv_local, slots, head_dim),
            block(kv_local, slots, head_dim),
        ],
        out_specs=block(kv_local, query_rows, head_dim),
        compiler_params=pltpu.CompilerParams(vmem_limit_bytes=VMEM_BYTES),
    )(lengths, q, entries, keys, values)


def angles(positions, steps, head_dim):
    freq_index = jnp.arange(head_dim // 2, dtype=jnp.float32)
    inverse_freq = jnp.exp(freq_index * (-2.0 * math.log(500000.0) / head_dim))
    step_pos = positions[None, :] + jnp.arange(steps, dtype=jnp.int32)[:, None]
    phase = step_pos.astype(jnp.float32)[..., None] * inverse_freq
    return jnp.cos(phase), jnp.sin(phase)


def body(n, hidden, w_query, key_value_weight, w_out, cache_keys, stored_values, lengths, positions):
    steps, row_local, depth = hidden.shape
    kv_local, head_dim = cache_keys.shape[1], cache_keys.shape[3]
    rows = steps * row_local
    ny = 2 if n == 8 else 1
    chunks = 4
    heads_local = w_out.shape[0] // head_dim
    group = heads_local // kv_local
    half = n // 2

    cosine, sine = angles(positions, steps, head_dim)
    tab = jnp.concatenate([cosine, cosine, -sine, sine], axis=-1).reshape(rows, 2 * head_dim)
    x = hidden.reshape(rows, 2, chunks, depth // (2 * chunks)).transpose(2, 1, 0, 3)
    x = x.reshape(chunks, 2 * rows, depth // (2 * chunks))
    kvcols = key_value_weight.shape[1]
    w_kv = key_value_weight
    if kvcols % 128:
        w_kv = jnp.pad(w_kv, ((0, 0), (0, 128 - kvcols % 128)))
    q, kv = project(ny, n, x, tab, w_query, w_kv)

    kv = kv[:, :, :kvcols].transpose(1, 0, 2).reshape(steps, row_local, kv_local, 2, head_dim)
    key, value = kv[:, :, :, 0], kv[:, :, :, 1]
    lower, upper = key[..., : head_dim // 2], key[..., head_dim // 2 :]
    cosine, sine = cosine[:, :, None], sine[:, :, None]
    key = jnp.concatenate([lower * cosine - upper * sine, upper * cosine + lower * sine], axis=-1)
    entries = jnp.stack([key, value], axis=3).astype(jnp.bfloat16)

    q = q.reshape(kv_local, group, steps, row_local, head_dim).transpose(3, 0, 2, 1, 4)
    q = q.reshape(row_local, kv_local, steps * group, head_dim)
    fresh = entries.transpose(1, 2, 3, 0, 4).reshape(row_local, kv_local, 2 * steps, head_dim)
    attended = attend(lengths, q, fresh.astype(jnp.float32), cache_keys, stored_values)

    wide = heads_local * head_dim
    a = attended.reshape(row_local, kv_local, steps, group * head_dim).transpose(2, 0, 1, 3)
    a = a.reshape(rows, 2, chunks, wide // (2 * chunks)).transpose(2, 1, 0, 3)
    a = a.reshape(chunks, 2 * rows, wide // (2 * chunks))
    out = mix(ny, n, a, w_out)
    out = out.reshape(n, steps, row_local, -1).transpose(1, 0, 2, 3)
    return out.reshape(steps, n * row_local, -1), entries


def solution(mesh):
    placed = (
        P(None, ("grp", "yz"), "gx"),
        P("gx", "yz"),
        P("gx", "yz"),
        P("gx", "yz"),
        P(("grp", "yz"), "gx", None, None),
        P(("grp", "yz"), "gx", None, None),
        P(("grp", "yz")),
        P(("grp", "yz")),
    )
    return jax.shard_map(
        functools.partial(body, mesh.shape["yz"]),
        mesh=mesh,
        in_specs=placed,
        out_specs=(P(None, "grp", ("yz", "gx")), P(None, ("grp", "yz"), "gx", None, None)),
        check_vma=False,
    )
```

```python
import functools
import math

import jax
import jax.numpy as jnp
from jax import lax
from jax.experimental import pallas as pl
from jax.experimental.pallas import tpu as pltpu
from jax.sharding import PartitionSpec as P

MESH = pl.DeviceIdType.MESH
VMEM_BYTES = 60 * 1024 * 1024
F32, BF16 = jnp.float32, jnp.bfloat16


def remote(src, dst, send, recv, **where):
    return pltpu.make_async_remote_copy(
        src_ref=src, dst_ref=dst, send_sem=send, recv_sem=recv, device_id=where, device_id_type=MESH
    )


def start(copy):
    copy.start()


def enter(n):
    me, core = lax.axis_index("yz"), lax.axis_index("gx")
    barrier = pltpu.get_barrier_semaphore()
    for k in range(1, 2 * n):
        there = lax.rem(me * 2 + core + k, 2 * n)
        pl.semaphore_signal(
            barrier,
            inc=1,
            device_id={"yz": lax.div(there, 2), "gx": lax.rem(there, 2)},
            device_id_type=MESH,
        )
    pl.semaphore_wait(barrier, 2 * n - 1)


class Gather:
    def __init__(self, ny, n, blocks, y_first, send, recv):
        self.ny, self.nz, self.n = ny, n // ny, n
        self.blocks, self.send, self.recv = blocks, send, recv
        self.y_first = y_first if ny == 2 else ()
        self.me = lax.axis_index("yz")
        self.z, self.y = lax.div(self.me, ny), lax.rem(self.me, ny)

    def copy(self, c, d, way):
        to = (self.me + 1 - 2 * self.y, self.me + self.ny, self.me - self.ny)[way]
        block = self.blocks[c].at[d]
        return remote(block, block, self.send.at[c, d, way], self.recv.at[c, d], yz=to)

    def await_block(self, c, d):
        block = self.blocks[c].at[d]
        remote(block, block, self.send.at[c, d, 0], self.recv.at[c, d], yz=self.me).wait_recv()

    def both_ways(self, c, d, act):
        @pl.when(self.z + 1 < self.nz)
        def _():
            act(self.copy(c, d, 1))

        @pl.when(self.z > 0)
        def _():
            act(self.copy(c, d, 2))

    def own(self, c, act):
        if c in self.y_first:
            act(self.copy(c, self.me, 0))
        self.both_ways(c, self.me, act)
        if self.ny == 2 and c not in self.y_first:
            act(self.copy(c, self.me, 0))

    def partner(self, c, act, wait):
        if c in self.y_first:
            d = self.z * 2 + 1 - self.y
            if wait:
                self.await_block(c, d)
            self.both_ways(c, d, act)

    def hop(self, c, s, act, wait):
        for sign in (1, -1):
            origin = self.z - sign * s
            onward = self.z + sign

            @pl.when((origin >= 0) & (origin < self.nz))
            def _():
                columns = (self.y, 1 - self.y) if c in self.y_first else (self.y,)
                for y in columns:
                    d = origin * self.ny + y
                    if wait:
                        self.await_block(c, d)

                    @pl.when((onward >= 0) & (onward < self.nz))
                    def _():
                        act(self.copy(c, d, 1 if sign > 0 else 2))

                    if self.ny == 2 and c not in self.y_first:
                        act(self.copy(c, d, 0))

    def across(self, c):
        if self.ny == 2 and c not in self.y_first:
            for z in range(self.nz):
                self.await_block(c, z * 2 + 1 - self.y)

    def finish(self):
        for c in range(len(self.blocks)):
            self.own(c, lambda copy: copy.wait_send())
            self.partner(c, lambda copy: copy.wait_send(), False)
            for s in range(1, self.nz):
                self.hop(c, s, lambda copy: copy.wait_send(), False)

    def steps(self, c):
        todo = [functools.partial(self.partner, c, start, True)] if c in self.y_first else []
        return todo + [
            functools.partial(self.hop, c, s, start, True) for s in range(1, self.nz)
        ]

    def weave(self, steps, work):
        steps, work = list(steps), list(work)
        each = -(-len(work) // max(1, len(steps)))
        for step in steps:
            step()
            for piece in work[:each]:
                piece()
            work = work[each:]
        for piece in work:
            piece()


def stacked(blocks, c, first, count, half):
    rows = blocks[c].shape[1] // 2
    block = blocks[c][pl.ds(first, count)].astype(F32)[:, half * rows : (half + 1) * rows, :]
    return block.reshape(count * rows, blocks[c].shape[2]).astype(BF16)


def kernel(
    ny, n, widths, y_first, widths2, y_first2, kv_cols, *refs
):
    (hid, freq, pos, lens, w_q, w_kv, w_o, keys_hbm, values_hbm, out, entries_out) = refs[:11]
    count, count2 = len(widths), len(widths2)
    blocks, blocks2 = refs[11 : 11 + count], refs[11 + count : 11 + count + count2]
    (
        wq, wkv, wo, keys, values, lhs, stage, tab, tabs, acc_q, acc_kv, got_q, got_kv,
        q_send, kv_send, q_recv, kv_recv, qf, af, ent, acc, got, wide,
        send, recv, send2, recv2, w_sem, o_sem, cache_sem, t_send, t_recv, p_send, p_recv,
        a_send, a_recv, s_send, s_recv,
    ) = refs[11 + count + count2 :]
    me, core = lax.axis_index("yz"), lax.axis_index("gx")
    half = n // 2
    steps, row_local = hid.shape[0], hid.shape[1]
    rows = steps * row_local
    mine, other = core * half, (1 - core) * half
    side, slot = lax.div(me, half), lax.rem(me, half)
    heads = wq.shape[1] // 128
    kv_local = keys.shape[1]
    group = half * heads // kv_local

    starts, starts2 = [0], [0]
    for w in widths:
        starts.append(starts[-1] + 2 * w)
    for w in widths2:
        starts2.append(starts2[-1] + 2 * w)

    def weight(c, which):
        part = pl.ds(starts[c], 2 * widths[c])
        src, dst = ((w_q, wq), (w_kv, wkv))[which]
        return pltpu.make_async_copy(src.at[part], dst.at[part], w_sem.at[c, which])

    def out_weight(c):
        part = pl.ds(starts2[c], 2 * widths2[c])
        return pltpu.make_async_copy(w_o.at[part], wo.at[part], o_sem.at[c])

    def cache(which):
        src, dst = ((keys_hbm, keys), (values_hbm, values))[which]
        return pltpu.make_async_copy(src, dst, cache_sem.at[which])

    for c in range(count):
        for which in range(2):
            weight(c, which).start()

    gather = Gather(ny, n, blocks, y_first, send, recv)
    gather2 = Gather(ny, n, blocks2, y_first2, send2, recv2)

    def place(c):
        w = widths[c]
        for h in range(2):
            for s in range(steps):
                at = h * rows + s * row_local
                part = hid[s, :, starts[c] + h * w : starts[c] + (h + 1) * w]
                stage[at : at + row_local, :w] = part.astype(F32)
        blocks[c][me] = stage[:, :w].astype(BF16)

    place(0)
    enter(n)
    gather.own(0, start)
    place(1)
    gather.own(1, start)

    row = lax.broadcasted_iota(jnp.int32, (rows, 128), 0)
    step_pos = jnp.zeros((rows, 128), F32)
    for s in range(steps):
        for b in range(row_local):
            step_pos = jnp.where(row == s * row_local + b, (pos[b] + s).astype(F32), step_pos)
    phase = step_pos * freq[...]
    lower = lax.broadcasted_iota(jnp.int32, (rows, 128), 1) < 64
    sine = jnp.sin(phase)
    tab[:, :128] = jnp.cos(phase)
    tab[:, 128:] = jnp.where(lower, -sine, sine)

    def tab_copy(k):
        return remote(tab, tabs.at[slot], t_send.at[k - 1], t_recv.at[slot], yz=lax.rem(me + k, n))

    @pl.when(side == core)
    def _():
        tabs[slot] = tab[...]
        for k in range(1, n):
            tab_copy(k).start()

    for which in range(2):
        cache(which).start()
    for c in range(count2):
        out_weight(c).start()
    for c in range(2, count):
        place(c)

    def add(ref, c, at, value):
        if c == 0:
            ref[at] = value
        else:
            ref[at] += value

    def load_lhs(c):
        gather.across(c)
        for which in range(2):
            weight(c, which).wait()
        for h in range(2):
            lhs[h, :, : widths[c]] = stacked(blocks, c, 0, n, h)

    def times(first, left, ref, cols):
        total = None
        for h in range(2):
            w = left[h].shape[1]
            part = slice(first + h * w, first + (h + 1) * w)
            term = jnp.dot(left[h], ref[part, cols], preferred_element_type=F32)
            total = term if h == 0 else total + term
        return total

    def piece(c, acc_ref, ref, cols):
        left = [lhs[h, :, : widths[c]] for h in range(2)]
        add(acc_ref, c, (slice(None), cols), times(starts[c], left, ref, cols))

    qcols, kvw = wq.shape[1], wkv.shape[1]

    def pieces(c):
        cut = qcols // 2
        return [
            functools.partial(load_lhs, c),
            functools.partial(piece, c, acc_q, wq, slice(0, cut)),
            functools.partial(piece, c, acc_q, wq, slice(cut, qcols)),
            functools.partial(piece, c, acc_kv, wkv, slice(0, kvw)),
        ]

    for c in range(count):
        if c + 1 < count and c > 0:
            gather.own(c + 1, start)
        gather.weave(gather.steps(c), pieces(c - 1) if c > 0 else [])

    last = count - 1
    gather.across(last)
    for which in range(2):
        weight(last, which).wait()

    def last_part(first):
        left = [stacked(blocks, last, first, half, h) for h in range(2)]
        part = pl.ds(pl.multiple_of(first * rows, 8), half * rows)
        acc_q[part] += times(starts[last], left, wq, slice(0, qcols))
        acc_kv[part] += times(starts[last], left, wkv, slice(0, kvw))

    theirs = pl.ds(pl.multiple_of(other * rows, 8), half * rows)
    swap_q = remote(acc_q.at[theirs], got_q, p_send.at[0], p_recv.at[0], gx=1 - core)
    swap_kv = remote(acc_kv.at[theirs], got_kv, p_send.at[1], p_recv.at[1], gx=1 - core)
    last_part(other)
    swap_q.start()
    swap_kv.start()
    last_part(mine)

    for i in range(half):
        @pl.when(mine + i != me)
        def _():
            remote(tab, tabs.at[i], t_send.at[0], t_recv.at[i], yz=me).wait_recv()

    swap_q.wait_recv()
    swap_kv.wait_recv()

    def moved(i, which):
        src, dst = ((q_send, q_recv), (kv_send, kv_recv))[which]
        return remote(
            src.at[i], dst.at[slot], a_send.at[which, i], a_recv.at[which, slot], yz=mine + i, gx=side
        )

    for i in range(half):
        own_rows = pl.ds(pl.multiple_of((mine + i) * rows, 8), rows)
        got_rows = slice(i * rows, (i + 1) * rows)
        turned = []
        for head in range(heads):
            cols = slice(head * 128, (head + 1) * 128)
            u = acc_q[own_rows, cols] + got_q[got_rows, cols]
            turned.append(u * tabs[i, :, :128] + pltpu.roll(u, 64, 1) * tabs[i, :, 128:])
            if head % 2 == 1:
                pair = jnp.concatenate(turned[-2:], axis=0).astype(BF16)
                q_send[i, (head - 1) * rows : (head + 1) * rows, :] = pair
        kv_send[i] = acc_kv[own_rows, :] + got_kv[got_rows, :]
        here = (mine + i == me) & (side == core)

        @pl.when(jnp.logical_not(here))
        def _():
            moved(i, 0).start()
            moved(i, 1).start()

        @pl.when(here)
        def _():
            q_recv[slot] = q_send[i]
            kv_recv[slot] = kv_send[i]

    def await_moved(j):
        @pl.when(jnp.logical_not((mine + j == me) & (side == core)))
        def _():
            remote(q_send.at[0], q_recv.at[j], a_send.at[0, 0], a_recv.at[0, j], yz=me).wait_recv()
            remote(kv_send.at[0], kv_recv.at[j], a_send.at[1, 0], a_recv.at[1, j], yz=me).wait_recv()

    per_vector = 128 // kv_cols
    per_head = half // kv_local
    for which in range(2):
        cache(which).wait()
    for j in range(half):
        await_moved(j)
    for i in range(2 * kv_local):
        parts = [kv_recv[i * per_vector + k, :, :kv_cols] for k in range(per_vector)]
        u = parts[0] if per_vector == 1 else jnp.concatenate(parts, axis=1)
        if i % 2 == 0:
            u = u * tab[:, :128] + pltpu.roll(u, 64, 1) * tab[:, 128:]
        u = u.astype(BF16)
        entries_out[:, i * 128 : (i + 1) * 128] = u
        ent[i] = u.astype(F32)
    for j in range(half):
        qf[j * heads * rows : (j + 1) * heads * rows, :] = q_recv[j].astype(F32)

    query_rows = steps * group
    slots = keys.shape[2]
    scale = 128 ** (-0.5)
    at_slot = lax.broadcasted_iota(jnp.int32, (query_rows, slots), 1)
    first_step = lax.broadcasted_iota(jnp.int32, (query_rows, 1), 0) < group

    def attend(h, b):
        base = h * group * rows
        picked = [pl.ds(base + s * row_local + b, group, stride=rows) for s in range(steps)]
        query_wide = jnp.concatenate([qf[p, :] for p in picked], axis=0)
        scores = lax.dot_general(
            query_wide.astype(BF16), keys[b, h], (((1,), (1,)), ((), ())), preferred_element_type=F32
        ) * scale
        scores = jnp.where(at_slot < lens[b], scores, -jnp.inf)
        key0, key1 = ent[2 * h, pl.ds(b, 1), :], ent[2 * h, pl.ds(row_local + b, 1), :]
        value0 = ent[2 * h + 1, pl.ds(b, 1), :]
        value1 = ent[2 * h + 1, pl.ds(row_local + b, 1), :]
        new0 = jnp.sum(query_wide * key0, axis=1, keepdims=True) * scale
        new1 = jnp.sum(query_wide * key1, axis=1, keepdims=True) * scale
        new1 = jnp.where(first_step, -jnp.inf, new1)
        top = jnp.maximum(jnp.max(scores, axis=1, keepdims=True), jnp.maximum(new0, new1))
        grown = jnp.exp(scores - top)
        grown0, grown1 = jnp.exp(new0 - top), jnp.exp(new1 - top)
        total = jnp.sum(grown, axis=1, keepdims=True) + (grown0 + grown1)
        weights = (grown / total).astype(BF16)
        weight0 = (grown0 / total).astype(BF16).astype(F32)
        weight1 = (grown1 / total).astype(BF16).astype(F32)
        result = jnp.dot(weights, values[b, h], preferred_element_type=F32)
        result = result + (weight0 * value0 + weight1 * value1)
        for s in range(steps):
            af[picked[s], :] = result[s * group : (s + 1) * group]

    def attend_rows(h, first, stop):
        @pl.loop(first, stop)
        def _(b):
            attend(h, b)

    def place2(c):
        w = widths2[c]
        for k in range(w // 128):
            top, bottom = starts2[c] // 128 + k, (starts2[c] + w) // 128 + k
            pair = [af[j * rows : (j + 1) * rows, :] for j in (top, bottom)]
            blocks2[c][me, :, k * 128 : (k + 1) * 128] = jnp.concatenate(pair, axis=0).astype(BF16)

    def load_lhs2(c):
        gather2.across(c)
        out_weight(c).wait()
        for h in range(2):
            lhs[h, :, : widths2[c]] = stacked(blocks2, c, 0, n, h)

    cut = acc.shape[2]

    def piece2(c, at):
        left = [lhs[h, :, : widths2[c]] for h in range(2)]
        whose = core if at < 2 else 1 - core
        cols = pl.ds(pl.multiple_of((whose * 2 + at % 2) * cut, 128), cut)
        add(acc, c, at, times(starts2[c], left, wo, cols))

    def pieces2(c):
        return [functools.partial(load_lhs2, c)] + [
            functools.partial(piece2, c, at) for at in (2, 3, 0, 1)
        ]

    swap = [remote(acc.at[2 + k], got.at[k], s_send.at[k], s_recv.at[k], gx=1 - core) for k in range(2)]

    ready = 0

    def send_ready(units):
        nonlocal ready
        while ready < count2 and starts2[ready + 1] <= units * 128:
            place2(ready)
            gather2.own(ready, start)
            ready += 1

    third = -(-row_local // 4)
    for h in range(kv_local):
        passing = gather2.steps(0) if ready > 0 else []
        work = [
            functools.partial(attend_rows, h, k, min(k + third, row_local))
            for k in range(0, row_local, third)
        ]
        work[0]()
        if passing:
            gather2.weave(passing, work[1:])
        else:
            for part in work[1:]:
                part()
        send_ready((h + 1) * group)

    for c in range(1, count2):
        gather2.weave(gather2.steps(c), pieces2(c - 1))
    last = count2 - 1
    load_lhs2(last)
    for at in (2, 3):
        piece2(last, at)
        swap[at - 2].start()
    piece2(last, 0)
    piece2(last, 1)
    for k in range(2):
        swap[k].wait_recv()
        cols = slice(k * cut, (k + 1) * cut)
        for d in range(n):
            for s in range(steps):
                at = slice(d * rows + s * row_local, d * rows + (s + 1) * row_local)
                wide[s, d * row_local : (d + 1) * row_local, cols] = acc[k, at, :] + got[k, at, :]
    for s in range(steps):
        out[s] = wide[s].astype(BF16)

    gather.finish()
    gather2.finish()
    swap_q.wait_send()
    swap_kv.wait_send()
    for k in range(2):
        swap[k].wait_send()

    @pl.when(side == core)
    def _():
        for k in range(1, n):
            tab_copy(k).wait_send()

    for i in range(half):
        @pl.when(jnp.logical_not((mine + i == me) & (side == core)))
        def _():
            moved(i, 0).wait_send()
            moved(i, 1).wait_send()


def body(n, hidden, w_query, key_value_weight, w_out, cache_keys, stored_values, lengths, positions):
    steps, row_local, depth = hidden.shape
    kv_local, head_dim = cache_keys.shape[1], cache_keys.shape[3]
    rows = steps * row_local
    ny = 2 if n == 8 else 1
    half = n // 2
    depth2, width = w_out.shape
    kv_cols = key_value_weight.shape[1]
    w_kv = key_value_weight
    if kv_cols % 128:
        w_kv = jnp.pad(w_kv, ((0, 0), (0, 128 - kv_cols % 128)))
    qcols, kvw = w_query.shape[1], w_kv.shape[1]
    heads = qcols // 128
    heads_local = depth2 // 128

    units = depth // 256
    tail = max(1, units // 6)
    big = -(-(units - tail) // 3)
    widths = [128 * w for w in (big, big, units - tail - 2 * big, tail)]
    units = depth2 // 256
    tail = max(1, round(units / 6))
    widths2 = [128 * w for w in (units // 2, units - units // 2 - tail, tail)]

    freq_index = jnp.arange(head_dim // 2, dtype=F32)
    inverse_freq = jnp.exp(freq_index * (-2.0 * math.log(500000.0) / head_dim))
    freq = jnp.concatenate([inverse_freq, inverse_freq])[None, :]

    dma = pltpu.SemaphoreType.DMA
    vmem = pl.BlockSpec(memory_space=pltpu.VMEM)
    smem = pl.BlockSpec(memory_space=pltpu.SMEM)
    hbm = pl.BlockSpec(memory_space=pl.ANY)
    count, count2 = len(widths), len(widths2)
    blocks = [pltpu.VMEM((n, 2 * rows, w), BF16) for w in widths + widths2]
    scratch = blocks + [
        pltpu.VMEM(w_query.shape, BF16),
        pltpu.VMEM(w_kv.shape, BF16),
        pltpu.VMEM(w_out.shape, BF16),
        pltpu.VMEM(cache_keys.shape, BF16),
        pltpu.VMEM(stored_values.shape, BF16),
        pltpu.VMEM((2, n * rows, max(widths + widths2)), BF16),
        pltpu.VMEM((2 * rows, max(widths)), F32),
        pltpu.VMEM((rows, 256), F32),
        pltpu.VMEM((half, rows, 256), F32),
        pltpu.VMEM((n * rows, qcols), F32),
        pltpu.VMEM((n * rows, kvw), F32),
        pltpu.VMEM((half * rows, qcols), F32),
        pltpu.VMEM((half * rows, kvw), F32),
        pltpu.VMEM((half, heads * rows, 128), BF16),
        pltpu.VMEM((half, rows, kvw), F32),
        pltpu.VMEM((half, heads * rows, 128), BF16),
        pltpu.VMEM((half, rows, kvw), F32),
        pltpu.VMEM((heads_local * rows, 128), F32),
        pltpu.VMEM((heads_local * rows, 128), F32),
        pltpu.VMEM((2 * kv_local, rows, 128), F32),
        pltpu.VMEM((4, n * rows, width // 4), F32),
        pltpu.VMEM((2, n * rows, width // 4), F32),
        pltpu.VMEM((steps, n * row_local, width // 2), F32),
        dma((count, n, 3)),
        dma((count, n)),
        dma((count2, n, 3)),
        dma((count2, n)),
        dma((count, 2)),
        dma((count2,)),
        dma((2,)),
        dma((n - 1,)),
        dma((half,)),
        dma((2,)),
        dma((2,)),
        dma((2, half)),
        dma((2, half)),
        dma((2,)),
        dma((2,)),
    ]
    out, entries = pl.pallas_call(
        functools.partial(
            kernel, ny, n, widths, (count - 1,), widths2, (count2 - 1,), min(kv_cols, 128)
        ),
        out_shape=(
            jax.ShapeDtypeStruct((steps, n * row_local, width // 2), BF16),
            jax.ShapeDtypeStruct((rows, 2 * kv_local * 128), BF16),
        ),
        in_specs=[vmem, vmem, smem, smem, hbm, hbm, hbm, hbm, hbm],
        out_specs=(vmem, vmem),
        scratch_shapes=scratch,
        compiler_params=pltpu.CompilerParams(
            collective_id=0, has_side_effects=True, vmem_limit_bytes=VMEM_BYTES
        ),
    )(hidden, freq, positions, lengths, w_query, w_kv, w_out, cache_keys, stored_values)
    return out, entries.reshape(steps, row_local, kv_local, 2, head_dim)


def solution(mesh):
    placed = (
        P(None, ("grp", "yz"), "gx"),
        P("gx", "yz"),
        P("gx", "yz"),
        P("gx", "yz"),
        P(("grp", "yz"), "gx", None, None),
        P(("grp", "yz"), "gx", None, None),
        P(("grp", "yz")),
        P(("grp", "yz")),
    )
    return jax.shard_map(
        functools.partial(body, mesh.shape["yz"]),
        mesh=mesh,
        in_specs=placed,
        out_specs=(P(None, "grp", ("yz", "gx")), P(None, ("grp", "yz"), "gx", None, None)),
        check_vma=False,
    )
```

```python
import functools
import math

import jax
import jax.numpy as jnp
from jax import lax
from jax.experimental import pallas as pl
from jax.experimental.pallas import tpu as pltpu
from jax.sharding import PartitionSpec as P

MESH = pl.DeviceIdType.MESH
VMEM_BYTES = 60 * 1024 * 1024
F32, BF16 = jnp.float32, jnp.bfloat16


def remote(src, dst, send, recv, **where):
    return pltpu.make_async_remote_copy(
        src_ref=src, dst_ref=dst, send_sem=send, recv_sem=recv, device_id=where, device_id_type=MESH
    )


def start(copy):
    copy.start()


def enter(n):
    me, core = lax.axis_index("yz"), lax.axis_index("gx")
    barrier = pltpu.get_barrier_semaphore()
    for k in range(1, 2 * n):
        there = lax.rem(me * 2 + core + k, 2 * n)
        pl.semaphore_signal(
            barrier,
            inc=1,
            device_id={"yz": lax.div(there, 2), "gx": lax.rem(there, 2)},
            device_id_type=MESH,
        )
    pl.semaphore_wait(barrier, 2 * n - 1)


class Gather:
    def __init__(self, ny, n, blocks, y_first, send, recv):
        self.ny, self.nz, self.n = ny, n // ny, n
        self.blocks, self.send, self.recv = blocks, send, recv
        self.y_first = y_first if ny == 2 else ()
        self.me = lax.axis_index("yz")
        self.z, self.y = lax.div(self.me, ny), lax.rem(self.me, ny)

    def copy(self, c, d, way):
        to = (self.me + 1 - 2 * self.y, self.me + self.ny, self.me - self.ny)[way]
        block = self.blocks[c].at[d]
        return remote(block, block, self.send.at[c, d, way], self.recv.at[c, d], yz=to)

    def await_block(self, c, d):
        block = self.blocks[c].at[d]
        remote(block, block, self.send.at[c, d, 0], self.recv.at[c, d], yz=self.me).wait_recv()

    def both_ways(self, c, d, act):
        @pl.when(self.z + 1 < self.nz)
        def _():
            act(self.copy(c, d, 1))

        @pl.when(self.z > 0)
        def _():
            act(self.copy(c, d, 2))

    def own(self, c, act):
        if c in self.y_first:
            act(self.copy(c, self.me, 0))
        self.both_ways(c, self.me, act)
        if self.ny == 2 and c not in self.y_first:
            act(self.copy(c, self.me, 0))

    def partner(self, c, act, wait):
        if c in self.y_first:
            d = self.z * 2 + 1 - self.y
            if wait:
                self.await_block(c, d)
            self.both_ways(c, d, act)

    def hop(self, c, s, act, wait):
        for sign in (1, -1):
            origin = self.z - sign * s
            onward = self.z + sign

            @pl.when((origin >= 0) & (origin < self.nz))
            def _():
                columns = (self.y, 1 - self.y) if c in self.y_first else (self.y,)
                for y in columns:
                    d = origin * self.ny + y
                    if wait:
                        self.await_block(c, d)

                    @pl.when((onward >= 0) & (onward < self.nz))
                    def _():
                        act(self.copy(c, d, 1 if sign > 0 else 2))

                    if self.ny == 2 and c not in self.y_first:
                        act(self.copy(c, d, 0))

    def across(self, c):
        if self.ny == 2 and c not in self.y_first:
            for z in range(self.nz):
                self.await_block(c, z * 2 + 1 - self.y)

    def finish(self):
        for c in range(len(self.blocks)):
            self.own(c, lambda copy: copy.wait_send())
            self.partner(c, lambda copy: copy.wait_send(), False)
            for s in range(1, self.nz):
                self.hop(c, s, lambda copy: copy.wait_send(), False)

    def steps(self, c):
        todo = [functools.partial(self.partner, c, start, True)] if c in self.y_first else []
        return todo + [
            functools.partial(self.hop, c, s, start, True) for s in range(1, self.nz)
        ]

    def weave(self, steps, work):
        steps, work = list(steps), list(work)
        each = -(-len(work) // max(1, len(steps)))
        for step in steps:
            step()
            for piece in work[:each]:
                piece()
            work = work[each:]
        for piece in work:
            piece()


def stacked(blocks, c, first, count, half):
    rows = blocks[c].shape[1] // 2
    block = blocks[c][pl.ds(first, count)].astype(F32)[:, half * rows : (half + 1) * rows, :]
    return block.reshape(count * rows, blocks[c].shape[2]).astype(BF16)


def kernel(
    ny, n, widths, y_first, widths2, y_first2, kv_cols, *refs
):
    (hid, freq, pos, lens, w_q, w_kv, w_o, keys_hbm, values_hbm, out, entries_out) = refs[:11]
    count, count2 = len(widths), len(widths2)
    blocks, blocks2 = refs[11 : 11 + count], refs[11 + count : 11 + count + count2]
    (
        wq, wkv, wo, keys, values, lhs, stage, tab, tabs, acc_q, acc_kv, got_q, got_kv,
        q_send, kv_send, q_recv, kv_recv, qf, af, ent, acc, got, wide,
        send, recv, send2, recv2, w_sem, o_sem, cache_sem, t_send, t_recv, p_send, p_recv,
        a_send, a_recv, s_send, s_recv,
    ) = refs[11 + count + count2 :]
    me, core = lax.axis_index("yz"), lax.axis_index("gx")
    half = n // 2
    steps, row_local = hid.shape[0], hid.shape[1]
    rows = steps * row_local
    mine, other = core * half, (1 - core) * half
    side, slot = lax.div(me, half), lax.rem(me, half)
    heads = wq.shape[1] // 128
    kv_local = keys.shape[1]
    group = half * heads // kv_local

    starts, starts2 = [0], [0]
    for w in widths:
        starts.append(starts[-1] + 2 * w)
    for w in widths2:
        starts2.append(starts2[-1] + 2 * w)

    def weight(c, which):
        part = pl.ds(starts[c], 2 * widths[c])
        src, dst = ((w_q, wq), (w_kv, wkv))[which]
        return pltpu.make_async_copy(src.at[part], dst.at[part], w_sem.at[c, which])

    def out_weight(c):
        part = pl.ds(starts2[c], 2 * widths2[c])
        return pltpu.make_async_copy(w_o.at[part], wo.at[part], o_sem.at[c])

    def cache(which):
        src, dst = ((keys_hbm, keys), (values_hbm, values))[which]
        return pltpu.make_async_copy(src, dst, cache_sem.at[which])

    gather = Gather(ny, n, blocks, y_first, send, recv)
    gather2 = Gather(ny, n, blocks2, y_first2, send2, recv2)

    def place(c):
        w = widths[c]
        for h in range(2):
            for s in range(steps):
                at = h * rows + s * row_local
                part = hid[s, :, starts[c] + h * w : starts[c] + (h + 1) * w]
                stage[at : at + row_local, :w] = part.astype(F32)
        blocks[c][me] = stage[:, :w].astype(BF16)

    place(0)
    enter(n)
    gather.own(0, start)
    place(1)
    gather.own(1, start)
    for which in range(2):
        weight(0, which).start()

    row = lax.broadcasted_iota(jnp.int32, (rows, 128), 0)
    step_pos = jnp.zeros((rows, 128), F32)
    for s in range(steps):
        for b in range(row_local):
            step_pos = jnp.where(row == s * row_local + b, (pos[b] + s).astype(F32), step_pos)
    phase = step_pos * freq[...]
    lower = lax.broadcasted_iota(jnp.int32, (rows, 128), 1) < 64
    sine = jnp.sin(phase)
    tab[:, :128] = jnp.cos(phase)
    tab[:, 128:] = jnp.where(lower, -sine, sine)

    def tab_copy(k):
        return remote(tab, tabs.at[slot], t_send.at[k - 1], t_recv.at[slot], yz=lax.rem(me + k, n))

    @pl.when(side == core)
    def _():
        tabs[slot] = tab[...]
        for k in range(1, n):
            tab_copy(k).start()

    for c in range(2, count):
        place(c)

    def add(ref, c, at, value):
        if c == 0:
            ref[at] = value
        else:
            ref[at] += value

    def load_lhs(c):
        gather.across(c)
        for which in range(2):
            weight(c, which).wait()
        for h in range(2):
            lhs[h, :, : widths[c]] = stacked(blocks, c, 0, n, h)

    def times(first, left, ref, cols):
        total = None
        for h in range(2):
            w = left[h].shape[1]
            part = slice(first + h * w, first + (h + 1) * w)
            term = jnp.dot(left[h], ref[part, cols], preferred_element_type=F32)
            total = term if h == 0 else total + term
        return total

    def piece(c, acc_ref, ref, cols):
        left = [lhs[h, :, : widths[c]] for h in range(2)]
        add(acc_ref, c, (slice(None), cols), times(starts[c], left, ref, cols))

    qcols, kvw = wq.shape[1], wkv.shape[1]

    def pieces(c):
        cut = qcols // 2
        return [
            functools.partial(load_lhs, c),
            functools.partial(piece, c, acc_q, wq, slice(0, cut)),
            functools.partial(piece, c, acc_q, wq, slice(cut, qcols)),
            functools.partial(piece, c, acc_kv, wkv, slice(0, kvw)),
        ]

    for c in range(count):
        if c + 1 < count and c > 0:
            gather.own(c + 1, start)
        if c + 1 < count:
            for which in range(2):
                weight(c + 1, which).start()
        if c == 1:
            for which in range(2):
                cache(which).start()
        if c == count - 1:
            for k in range(count2):
                out_weight(k).start()
        gather.weave(gather.steps(c), pieces(c - 1) if c > 0 else [])

    last = count - 1
    gather.across(last)
    for which in range(2):
        weight(last, which).wait()

    def last_part(first):
        left = [stacked(blocks, last, first, half, h) for h in range(2)]
        part = pl.ds(pl.multiple_of(first * rows, 8), half * rows)
        acc_q[part] += times(starts[last], left, wq, slice(0, qcols))
        acc_kv[part] += times(starts[last], left, wkv, slice(0, kvw))

    theirs = pl.ds(pl.multiple_of(other * rows, 8), half * rows)
    swap_q = remote(acc_q.at[theirs], got_q, p_send.at[0], p_recv.at[0], gx=1 - core)
    swap_kv = remote(acc_kv.at[theirs], got_kv, p_send.at[1], p_recv.at[1], gx=1 - core)
    last_part(other)
    swap_q.start()
    swap_kv.start()
    last_part(mine)

    for i in range(half):
        @pl.when(mine + i != me)
        def _():
            remote(tab, tabs.at[i], t_send.at[0], t_recv.at[i], yz=me).wait_recv()

    swap_q.wait_recv()
    swap_kv.wait_recv()

    def moved(i, which):
        src, dst = ((q_send, q_recv), (kv_send, kv_recv))[which]
        return remote(
            src.at[i], dst.at[slot], a_send.at[which, i], a_recv.at[which, slot], yz=mine + i, gx=side
        )

    for i in range(half):
        own_rows = pl.ds(pl.multiple_of((mine + i) * rows, 8), rows)
        got_rows = slice(i * rows, (i + 1) * rows)
        turned = []
        for head in range(heads):
            cols = slice(head * 128, (head + 1) * 128)
            u = acc_q[own_rows, cols] + got_q[got_rows, cols]
            turned.append(u * tabs[i, :, :128] + pltpu.roll(u, 64, 1) * tabs[i, :, 128:])
            if head % 2 == 1:
                pair = jnp.concatenate(turned[-2:], axis=0).astype(BF16)
                q_send[i, (head - 1) * rows : (head + 1) * rows, :] = pair
        kv_send[i] = acc_kv[own_rows, :] + got_kv[got_rows, :]
        here = (mine + i == me) & (side == core)

        @pl.when(jnp.logical_not(here))
        def _():
            moved(i, 0).start()
            moved(i, 1).start()

        @pl.when(here)
        def _():
            q_recv[slot] = q_send[i]
            kv_recv[slot] = kv_send[i]

    def await_moved(j):
        @pl.when(jnp.logical_not((mine + j == me) & (side == core)))
        def _():
            remote(q_send.at[0], q_recv.at[j], a_send.at[0, 0], a_recv.at[0, j], yz=me).wait_recv()
            remote(kv_send.at[0], kv_recv.at[j], a_send.at[1, 0], a_recv.at[1, j], yz=me).wait_recv()

    per_vector = 128 // kv_cols
    per_head = half // kv_local
    for which in range(2):
        cache(which).wait()
    for j in range(half):
        await_moved(j)
    for i in range(2 * kv_local):
        parts = [kv_recv[i * per_vector + k, :, :kv_cols] for k in range(per_vector)]
        u = parts[0] if per_vector == 1 else jnp.concatenate(parts, axis=1)
        if i % 2 == 0:
            u = u * tab[:, :128] + pltpu.roll(u, 64, 1) * tab[:, 128:]
        u = u.astype(BF16)
        entries_out[:, i * 128 : (i + 1) * 128] = u
        ent[i] = u.astype(F32)
    for j in range(half):
        qf[j * heads * rows : (j + 1) * heads * rows, :] = q_recv[j].astype(F32)

    query_rows = steps * group
    slots = keys.shape[2]
    scale = 128 ** (-0.5)
    at_slot = lax.broadcasted_iota(jnp.int32, (query_rows, slots), 1)
    first_step = lax.broadcasted_iota(jnp.int32, (query_rows, 1), 0) < group

    def attend(h, b):
        base = h * group * rows
        picked = [pl.ds(base + s * row_local + b, group, stride=rows) for s in range(steps)]
        query_wide = jnp.concatenate([qf[p, :] for p in picked], axis=0)
        scores = lax.dot_general(
            query_wide.astype(BF16), keys[b, h], (((1,), (1,)), ((), ())), preferred_element_type=F32
        ) * scale
        scores = jnp.where(at_slot < lens[b], scores, -jnp.inf)
        key0, key1 = ent[2 * h, pl.ds(b, 1), :], ent[2 * h, pl.ds(row_local + b, 1), :]
        value0 = ent[2 * h + 1, pl.ds(b, 1), :]
        value1 = ent[2 * h + 1, pl.ds(row_local + b, 1), :]
        new0 = jnp.sum(query_wide * key0, axis=1, keepdims=True) * scale
        new1 = jnp.sum(query_wide * key1, axis=1, keepdims=True) * scale
        new1 = jnp.where(first_step, -jnp.inf, new1)
        top = jnp.maximum(jnp.max(scores, axis=1, keepdims=True), jnp.maximum(new0, new1))
        grown = jnp.exp(scores - top)
        grown0, grown1 = jnp.exp(new0 - top), jnp.exp(new1 - top)
        total = jnp.sum(grown, axis=1, keepdims=True) + (grown0 + grown1)
        weights = (grown / total).astype(BF16)
        weight0 = (grown0 / total).astype(BF16).astype(F32)
        weight1 = (grown1 / total).astype(BF16).astype(F32)
        result = jnp.dot(weights, values[b, h], preferred_element_type=F32)
        result = result + (weight0 * value0 + weight1 * value1)
        for s in range(steps):
            af[picked[s], :] = result[s * group : (s + 1) * group]

    def attend_rows(h, first, stop):
        @pl.loop(first, stop)
        def _(b):
            attend(h, b)

    def place2(c):
        w = widths2[c]
        for k in range(w // 128):
            top, bottom = starts2[c] // 128 + k, (starts2[c] + w) // 128 + k
            pair = [af[j * rows : (j + 1) * rows, :] for j in (top, bottom)]
            blocks2[c][me, :, k * 128 : (k + 1) * 128] = jnp.concatenate(pair, axis=0).astype(BF16)

    def load_lhs2(c):
        gather2.across(c)
        out_weight(c).wait()
        for h in range(2):
            lhs[h, :, : widths2[c]] = stacked(blocks2, c, 0, n, h)

    cut = acc.shape[2]

    def piece2(c, at):
        left = [lhs[h, :, : widths2[c]] for h in range(2)]
        whose = core if at < 2 else 1 - core
        cols = pl.ds(pl.multiple_of((whose * 2 + at % 2) * cut, 128), cut)
        add(acc, c, at, times(starts2[c], left, wo, cols))

    def pieces2(c):
        return [functools.partial(load_lhs2, c)] + [
            functools.partial(piece2, c, at) for at in (2, 3, 0, 1)
        ]

    swap = [remote(acc.at[2 + k], got.at[k], s_send.at[k], s_recv.at[k], gx=1 - core) for k in range(2)]

    ready = 0

    def send_ready(units):
        nonlocal ready
        while ready < count2 and starts2[ready + 1] <= units * 128:
            place2(ready)
            gather2.own(ready, start)
            ready += 1

    third = -(-row_local // 4)
    for h in range(kv_local):
        passing = gather2.steps(0) if ready > 0 else []
        work = [
            functools.partial(attend_rows, h, k, min(k + third, row_local))
            for k in range(0, row_local, third)
        ]
        work[0]()
        if passing:
            gather2.weave(passing, work[1:])
        else:
            for part in work[1:]:
                part()
        send_ready((h + 1) * group)

    for c in range(1, count2):
        gather2.weave(gather2.steps(c), pieces2(c - 1))
    last = count2 - 1
    load_lhs2(last)
    for at in (2, 3):
        piece2(last, at)
        swap[at - 2].start()
    piece2(last, 0)
    piece2(last, 1)
    for k in range(2):
        swap[k].wait_recv()
        cols = slice(k * cut, (k + 1) * cut)
        for d in range(n):
            for s in range(steps):
                at = slice(d * rows + s * row_local, d * rows + (s + 1) * row_local)
                wide[s, d * row_local : (d + 1) * row_local, cols] = acc[k, at, :] + got[k, at, :]
    for s in range(steps):
        out[s] = wide[s].astype(BF16)

    gather.finish()
    gather2.finish()
    swap_q.wait_send()
    swap_kv.wait_send()
    for k in range(2):
        swap[k].wait_send()

    @pl.when(side == core)
    def _():
        for k in range(1, n):
            tab_copy(k).wait_send()

    for i in range(half):
        @pl.when(jnp.logical_not((mine + i == me) & (side == core)))
        def _():
            moved(i, 0).wait_send()
            moved(i, 1).wait_send()


def body(n, hidden, w_query, key_value_weight, w_out, cache_keys, stored_values, lengths, positions):
    steps, row_local, depth = hidden.shape
    kv_local, head_dim = cache_keys.shape[1], cache_keys.shape[3]
    rows = steps * row_local
    ny = 2 if n == 8 else 1
    half = n // 2
    depth2, width = w_out.shape
    kv_cols = key_value_weight.shape[1]
    w_kv = key_value_weight
    if kv_cols % 128:
        w_kv = jnp.pad(w_kv, ((0, 0), (0, 128 - kv_cols % 128)))
    qcols, kvw = w_query.shape[1], w_kv.shape[1]
    heads = qcols // 128
    heads_local = depth2 // 128

    units = depth // 256
    tail = max(1, units // 6)
    big = -(-(units - tail) // 3)
    widths = [128 * w for w in (big, big, units - tail - 2 * big, tail)]
    units = depth2 // 256
    tail = max(1, round(units / 6))
    widths2 = [128 * w for w in (units // 2, units - units // 2 - tail, tail)]

    freq_index = jnp.arange(head_dim // 2, dtype=F32)
    inverse_freq = jnp.exp(freq_index * (-2.0 * math.log(500000.0) / head_dim))
    freq = jnp.concatenate([inverse_freq, inverse_freq])[None, :]

    dma = pltpu.SemaphoreType.DMA
    vmem = pl.BlockSpec(memory_space=pltpu.VMEM)
    smem = pl.BlockSpec(memory_space=pltpu.SMEM)
    hbm = pl.BlockSpec(memory_space=pl.ANY)
    count, count2 = len(widths), len(widths2)
    blocks = [pltpu.VMEM((n, 2 * rows, w), BF16) for w in widths + widths2]
    scratch = blocks + [
        pltpu.VMEM(w_query.shape, BF16),
        pltpu.VMEM(w_kv.shape, BF16),
        pltpu.VMEM(w_out.shape, BF16),
        pltpu.VMEM(cache_keys.shape, BF16),
        pltpu.VMEM(stored_values.shape, BF16),
        pltpu.VMEM((2, n * rows, max(widths + widths2)), BF16),
        pltpu.VMEM((2 * rows, max(widths)), F32),
        pltpu.VMEM((rows, 256), F32),
        pltpu.VMEM((half, rows, 256), F32),
        pltpu.VMEM((n * rows, qcols), F32),
        pltpu.VMEM((n * rows, kvw), F32),
        pltpu.VMEM((half * rows, qcols), F32),
        pltpu.VMEM((half * rows, kvw), F32),
        pltpu.VMEM((half, heads * rows, 128), BF16),
        pltpu.VMEM((half, rows, kvw), F32),
        pltpu.VMEM((half, heads * rows, 128), BF16),
        pltpu.VMEM((half, rows, kvw), F32),
        pltpu.VMEM((heads_local * rows, 128), F32),
        pltpu.VMEM((heads_local * rows, 128), F32),
        pltpu.VMEM((2 * kv_local, rows, 128), F32),
        pltpu.VMEM((4, n * rows, width // 4), F32),
        pltpu.VMEM((2, n * rows, width // 4), F32),
        pltpu.VMEM((steps, n * row_local, width // 2), F32),
        dma((count, n, 3)),
        dma((count, n)),
        dma((count2, n, 3)),
        dma((count2, n)),
        dma((count, 2)),
        dma((count2,)),
        dma((2,)),
        dma((n - 1,)),
        dma((half,)),
        dma((2,)),
        dma((2,)),
        dma((2, half)),
        dma((2, half)),
        dma((2,)),
        dma((2,)),
    ]
    out, entries = pl.pallas_call(
        functools.partial(
            kernel, ny, n, widths, (count - 1,), widths2, (count2 - 1,), min(kv_cols, 128)
        ),
        out_shape=(
            jax.ShapeDtypeStruct((steps, n * row_local, width // 2), BF16),
            jax.ShapeDtypeStruct((rows, 2 * kv_local * 128), BF16),
        ),
        in_specs=[vmem, vmem, smem, smem, hbm, hbm, hbm, hbm, hbm],
        out_specs=(vmem, vmem),
        scratch_shapes=scratch,
        compiler_params=pltpu.CompilerParams(
            collective_id=0, has_side_effects=True, vmem_limit_bytes=VMEM_BYTES
        ),
    )(hidden, freq, positions, lengths, w_query, w_kv, w_out, cache_keys, stored_values)
    return out, entries.reshape(steps, row_local, kv_local, 2, head_dim)


def solution(mesh):
    placed = (
        P(None, ("grp", "yz"), "gx"),
        P("gx", "yz"),
        P("gx", "yz"),
        P("gx", "yz"),
        P(("grp", "yz"), "gx", None, None),
        P(("grp", "yz"), "gx", None, None),
        P(("grp", "yz")),
        P(("grp", "yz")),
    )
    return jax.shard_map(
        functools.partial(body, mesh.shape["yz"]),
        mesh=mesh,
        in_specs=placed,
        out_specs=(P(None, "grp", ("yz", "gx")), P(None, ("grp", "yz"), "gx", None, None)),
        check_vma=False,
    )
```
